1024 devices in a mesh: dp: 64 (over z, core), expert: 16 (over x, y).
Axes of the slice: x: 4, y: 4, z: 32, core: 2. Of those that a mesh axis runs over, the one named last changes fastest.
Arguments:
- out_grad: bfloat16 [49152, 2048], P(('dp', 'expert')), may hold values from -6 to 6
- probs: bfloat16 [49152, 8], P(('dp', 'expert')), may hold values from 0.049804688 to 0.5
- expert_ids: int32 [49152, 8], P(('dp', 'expert')), may hold values from 0 to 15, all different within a row; in each aligned block of 48 rows (0 to 47, 48 to 95, ...) at most 28 rows name the same one
- saved_pre: bfloat16 [458752, 1536], P(('dp', 'expert')), may hold values from -5 to 5
- down_weight: bfloat16 [16, 2048, 768], P('expert'), may hold values from -0.21875 to 0.21875
Outputs:
- grad_down: float32 [16, 2048, 768], P('expert', 'dp')
- grad_pre: bfloat16 [458752, 1536], P(('dp', 'expert'))
- grad_probs: float32 [49152, 8], P(('dp', 'expert'))
The draws below stay inside these ranges and needn't reach their ends.
Inputs may be any that keep to these rules, and one draw needn't show every extreme that they name: `expert_ids`: each row names 8 different experts; within the 48 tokens of one device no expert is named by more than 28 tokens, a bound that some block reaches of them.
All inputs are finite; a program needn't handle non-finite values.
Results may differ from the reference program's by a relative error of at most 0.007.
Values may be sent and summed in bfloat16 or wider, within the bound.
A program may use at most 64 MiB of HBM per device.

```python
import math
import jax
import jax.numpy as jnp
import numpy as np
from jax import lax

D = 2048
H = 768
EXPERTS = 16
TOP = 8
TOK_DEV = 48
CAP = 28
TOKENS = 49152
ROWS = 458752
N_DP = 64
N_EXPERT = 16


def strengthened(drawn, stream_key, source, target, parts, factor):
    def block_of(axis_at):
        return (jnp.arange(drawn.shape[axis_at]) // (drawn.shape[axis_at] // parts)).reshape((-1,) + (1,) * (drawn.ndim - 1 - axis_at))

    first = jax.random.permutation(stream_key, parts)[block_of(target)]
    far = (block_of(target) + parts // 2) % parts
    return jnp.where((block_of(source) == first) | (block_of(source) == far), factor * drawn, drawn)


def steps_of(own_key, dims, split, low, largest):
    factor_of, own = 1.0, jax.random.fold_in(own_key, 6)
    for axis_at, blocks in split:
        steps = jnp.exp(jax.random.uniform(jax.random.fold_in(own, axis_at), (blocks,), jnp.float32, low / len(split), largest / len(split)))
        factor_of = factor_of * jnp.repeat(steps, dims[axis_at] // blocks).reshape([-1 if axis == axis_at else 1 for axis in range(len(dims))])
    return factor_of


def deal_out(stream_key, own, number, rows, count, top, reach, slope):
    sequence = jax.random.permutation(stream_key, count)
    heavy_load, ordinary = portions_of(count, rows * top, reach, slope, True), portions_of(count, rows * top, reach, slope, False)
    places = jnp.arange(count)

    def named(lengths, offset_by):
        used = int((lengths > 0).sum())
        fixed = max(1, used // 4)
        moved = fixed + (places - fixed + offset_by * (used - fixed)) % max(1, count - fixed)
        return jnp.zeros((count,), jnp.int32).at[sequence[jnp.where(places < fixed, places, moved)]].set(jnp.asarray(lengths, jnp.int32))

    lengths = jnp.where(number % 4 == 0, named(heavy_load, number // 4), named(ordinary, number - number // 4 - 1))
    mixed = jax.random.permutation(jax.random.fold_in(own, 3), count)
    donor, receiver = mixed[0:count // 2 * 2:2], mixed[1:count // 2 * 2:2]
    room = jnp.minimum(lengths[donor] - 1, reach - lengths[receiver]) // 2
    room = jnp.where((donor == sequence[0]) | (receiver == sequence[0]) | (lengths[receiver] == 0), 0, jnp.maximum(room, 0))
    moved = jax.random.randint(jax.random.fold_in(own, 4), (count // 2,), 0, 1 << 20) % (room + 1)
    lengths = lengths.at[donor].add(-moved).at[receiver].add(moved)
    members = jnp.searchsorted(jnp.cumsum(lengths), jnp.arange(rows * top), side="right").astype(jnp.int32)
    listing = members.reshape(top, rows).T
    listing = listing[jax.random.permutation(jax.random.fold_in(own, 1), rows)]
    offset_by = jax.random.randint(jax.random.fold_in(own, 2), (rows, 1), 0, top)
    return jnp.take_along_axis(listing, (jnp.arange(top)[None, :] + offset_by) % top, axis=1)


def portions_of(amount, total, most, lean, full):
    loads = [(1 << 20) // math.isqrt(standing ** lean) + 1 for standing in range(1, amount + 1)]
    largest = most if full else min(most, max(-(-total // amount), total * loads[0] // sum(loads)))
    least = 1 if total - largest >= amount - 1 else 0
    given, rest = [largest] + [least] * (amount - 1), total - largest - least * (amount - 1)
    while rest > 0:
        free = [i for i in range(1, amount) if given[i] < largest] or [i for i in range(1, amount) if given[i] < most]
        mass, remaining = sum([loads[i] for i in free]), rest
        for i in free:
            addition = min(most - given[i], max(1, remaining * loads[i] // mass), rest)
            given[i] = given[i] + addition
            rest = rest - addition
    return np.array(given)


def bell_draw(stream_key, shape, spread, limit, split=(), kind=jnp.bfloat16):
    loudness = steps_of(stream_key, shape, split, -0.22, 0.18) if split else 1.0
    result = jax.random.normal(stream_key, shape, jnp.float32) * spread * loudness
    return jnp.minimum(jnp.maximum(result, -limit), limit).astype(kind)


def noise_with(key, shape, width, most, cuts, heavy, kind=jnp.bfloat16):
    drawn = width * jax.random.normal(key, shape, jnp.float32)
    if cuts:
        drawn = drawn * steps_of(key, shape, cuts, -0.22, 0.18)
    return jnp.clip(strengthened(drawn, jax.random.fold_in(key, 3), *heavy), -most, most).astype(kind)


def setup_inputs(seed: int = 0) -> dict:
    key_of = jax.random.split(jax.random.key(seed), 6)
    out_grad = noise_with(key_of[0], (TOKENS, D), 0.25, 6.0, ((0, 1024),), (0, 1, 1024, 6.0))
    probs = jnp.clip(jnp.exp(math.log(0.5) - 2.306499 * jax.random.uniform(key_of[1], (TOKENS, TOP), jnp.float32) ** steps_of(key_of[1], (TOKENS, TOP), ((0, 1024),), -0.2, 0.2)), 0.049804688, 0.5).astype(jnp.bfloat16)
    expert_ids_keys = jax.random.split(jax.random.fold_in(key_of[2], 1), TOKENS // TOK_DEV)
    expert_ids_turns = jax.random.permutation(jax.random.fold_in(key_of[2], 3), TOKENS // TOK_DEV)
    expert_ids = jax.vmap(lambda own, number: deal_out(jax.random.fold_in(key_of[2], 2), own, number, TOK_DEV, EXPERTS, TOP, CAP, 2))(expert_ids_keys, expert_ids_turns).reshape((TOKENS, TOP))
    saved_pre = bell_draw(key_of[3], (ROWS, 2 * H), 1.0, 5.0, ((0, 1024),))
    down_weight = bell_draw(key_of[4], (EXPERTS, D, H), H ** -0.5, 0.21875, ((0, 16),))
    return dict(out_grad=out_grad, probs=probs, expert_ids=expert_ids, saved_pre=saved_pre, down_weight=down_weight)


def slots_of(expert_ids):
    blocks = expert_ids.reshape(-1, TOK_DEV, TOP)
    onehot = (blocks[..., None] == jnp.arange(EXPERTS, dtype=jnp.int32)).astype(jnp.int32)
    per_token = jnp.sum(onehot, axis=2)
    before = jnp.cumsum(per_token, axis=1) - per_token
    slot_index = jnp.sum(onehot * before[:, :, None, :], axis=3)
    return slot_index.reshape(expert_ids.shape).astype(jnp.int32)


def reference(out_grad, probs, expert_ids, saved_pre, down_weight):
    slot_index = slots_of(expert_ids)
    group_tokens = N_EXPERT * TOK_DEV
    group_rows = N_EXPERT * CAP
    grads = out_grad.reshape(N_DP, group_tokens, D)
    weights = probs.reshape(N_DP, group_tokens, TOP)
    chosen = expert_ids.reshape(N_DP, group_tokens, TOP)
    slots = slot_index.reshape(N_DP, group_tokens, TOP)
    stored = saved_pre.reshape(N_DP, EXPERTS, group_rows, 2 * H)
    weight_f = down_weight.astype(jnp.float32)
    source = (jnp.arange(group_tokens, dtype=jnp.int32) // TOK_DEV)[:, None]

    def group_step(carry, pieces):
        grad_g, prob_g, chosen_g, slot_g, stored_g = pieces
        dest = (chosen_g * group_rows + source * CAP + slot_g).astype(jnp.int32)
        flat_dest = dest.reshape(-1)
        values = jnp.broadcast_to(grad_g[:, None, :], (group_tokens, TOP, D)).reshape(-1, D)
        routed = jnp.zeros((EXPERTS * group_rows, D), jnp.bfloat16).at[flat_dest].set(values)
        routed_p = jnp.zeros((EXPERTS * group_rows,), jnp.bfloat16).at[flat_dest].set(prob_g.reshape(-1))
        routed = routed.reshape(EXPERTS, group_rows, D)
        routed_p = routed_p.reshape(EXPERTS, group_rows, 1).astype(jnp.float32)
        stored_f = stored_g.astype(jnp.float32)
        gate_pre = stored_f[..., :H]
        up_pre = stored_f[..., H:]
        sigmoid_gate = jax.nn.sigmoid(gate_pre)
        hidden = (gate_pre * sigmoid_gate * up_pre).astype(jnp.bfloat16)
        scaled = (routed_p * routed.astype(jnp.float32)).astype(jnp.bfloat16)
        back_proj = jnp.einsum('erd,edh->erh', routed.astype(jnp.float32), weight_f)
        hidden_f = hidden.astype(jnp.float32)
        products = jnp.sum(hidden_f * back_proj, axis=2)
        grad_hidden = routed_p * back_proj
        grad_gate = grad_hidden * up_pre * sigmoid_gate * (1.0 + gate_pre * (1.0 - sigmoid_gate))
        grad_up = grad_hidden * gate_pre * sigmoid_gate
        grad_pre_g = jnp.concatenate([grad_gate, grad_up], axis=2).astype(jnp.bfloat16)
        weight_term = jnp.einsum('erd,erh->edh', scaled.astype(jnp.float32), hidden_f)
        grad_probs_g = products.reshape(-1)[flat_dest].reshape(group_tokens, TOP)
        return carry + weight_term, (grad_pre_g, grad_probs_g)

    start = jnp.zeros((EXPERTS, D, H), jnp.float32)
    grad_down, (grad_pre, grad_probs) = lax.scan(group_step, start, (grads, weights, chosen, slots, stored))
    return grad_down, grad_pre.reshape(ROWS, 2 * H), grad_probs.reshape(TOKENS, TOP)
```

```python
import jax
import jax.numpy as jnp
from jax import lax
from jax.experimental import pallas as pl
from jax.experimental.pallas import tpu as pltpu
from jax.sharding import PartitionSpec as P

MESH = pl.DeviceIdType.MESH
F32, BF16 = jnp.float32, jnp.bfloat16
SIDE = 4
OWNERS = 16
CHUNKS = 8
WIDTH = 256
HALF = 128
STEPS = 16
CHIPS = 32
SHARE = 32
SUBS = 2


def div(a, b):
    return lax.div(jnp.int32(a), jnp.int32(b))


def rem(a, b):
    return lax.rem(jnp.int32(a), jnp.int32(b))


def kernel(
    grad_hbm, probs_ref, ids_ref, stored_hbm, weight_hbm,
    down_ref, pre_hbm, gprobs_ref,
    g, w, stored, hidden, d_gate, d_up, back, routed_all, pre,
    pick, prob_col, cols, slot_tab, meta_out, meta_in, prod_out, prod_in,
    part, part_in, acc_out, acc_in,
    sem_g, sem_w, sem_stored, sem_pre, gs, gr, ms, mr, rs, rr, ss, sr, zs, zr,
):
    tok, top = ids_ref.shape
    rows = stored_hbm.shape[0]
    hid_n = weight_hbm.shape[2]
    cap = rows // OWNERS
    dp = lax.axis_index("dp")
    me = lax.axis_index("expert")
    z, core = div(dp, 2), rem(dp, 2)
    x, y = div(me, SIDE), rem(me, SIDE)
    odd = rem(z, 2)
    first_group = div(z + STEPS, 2)
    n_groups = 2 * CHUNKS
    up_z = (rem(z + 1, CHIPS) * 2 + core, me)
    down_z = (rem(z + CHIPS - 1, CHIPS) * 2 + core, me)
    sibling = (z * 2 + 1 - core, me)

    def own_coords(i):
        par = rem(i, 2)
        return par, y * (1 - par) + x * par, x * (1 - par) + y * par

    def group_of(i, half):
        par = rem(i, 2)
        start = (1 - par) * i - par * (i + 1)
        return rem(first_group + start + half + 2 * n_groups, n_groups)

    def load_g(i, half):
        _, u, v = own_coords(i)
        at = pl.multiple_of(group_of(i, half) * HALF, HALF)
        return pltpu.make_async_copy(
            grad_hbm.at[:, pl.ds(at, HALF)],
            g.at[i, u, v, :, pl.ds(half * HALF, HALF)],
            sem_g.at[i, half],
        )

    def load_w(i, half):
        at = pl.multiple_of(group_of(i, half) * HALF, HALF)
        return pltpu.make_async_copy(
            weight_hbm.at[0, pl.ds(at, HALF), :],
            w.at[i, pl.ds(half * HALF, HALF), :],
            sem_w.at[i, half],
        )

    for i in range(CHUNKS):
        for half in range(2):
            load_g(i, half).start()
    load_stored = pltpu.make_async_copy(stored_hbm, stored, sem_stored)
    load_stored.start()
    for i in range(CHUNKS):
        for half in range(2):
            load_w(i, half).start()

    barrier = pltpu.get_barrier_semaphore()

    def greet(j, carry):
        pl.semaphore_signal(barrier, inc=1, device_id=(dp, rem(me + j, OWNERS)), device_id_type=MESH)
        return carry

    for target in (up_z, down_z, sibling):
        pl.semaphore_signal(barrier, inc=1, device_id=target, device_id_type=MESH)
    lax.fori_loop(1, OWNERS, greet, 0)

    lane = lax.broadcasted_iota(jnp.int32, (tok, HALF), 1)
    chosen = jnp.zeros((tok, HALF), F32)
    prob = jnp.zeros((tok, HALF), F32)
    for k in range(top):
        hit = ids_ref[:, k : k + 1] == lane
        chosen = chosen + jnp.where(hit, 1.0, 0.0)
        prob = prob + jnp.where(hit, probs_ref[:, k : k + 1].astype(F32), 0.0)
    lower = (
        lax.broadcasted_iota(jnp.int32, (tok, tok), 0) > lax.broadcasted_iota(jnp.int32, (tok, tok), 1)
    )
    before = jnp.dot(
        jnp.where(lower, 1.0, 0.0).astype(BF16), chosen.astype(BF16), preferred_element_type=F32
    )
    slots = jnp.where(chosen > 0.0, before, -1.0)
    slot_tab[...] = slots
    fill = jnp.zeros((HALF - tok, HALF), F32)
    slots_t = jnp.concatenate([slots, fill - 1.0], axis=0).T
    prob_t = jnp.concatenate([prob, fill], axis=0).T
    sub8 = lax.broadcasted_iota(jnp.int32, (8, HALF), 0)
    for e in range(OWNERS):
        meta_out[e] = jnp.where(
            sub8 == 0,
            jnp.broadcast_to(slots_t[e : e + 1], (8, HALF)),
            jnp.broadcast_to(prob_t[e : e + 1], (8, HALF)),
        )
    meta_in[me] = meta_out[me]

    pl.semaphore_wait(barrier, OWNERS - 1 + 3)

    def move(i, k):
        par, u, v = own_coords(i)
        turn = rem(div(i, 2), 2)
        if k < 3:
            step = (1, SIDE - 1, None)[k]
            if k == 2:
                source, step = rem(v + SIDE - 1 + 2 * turn, SIDE), SIDE + 1 - 2 * turn
            else:
                source = v
            block = g.at[i, u, source]
            uu, vv = u, rem(v + step, SIDE)
        else:
            step = (1, SIDE - 1, None)[k - 3]
            if k == 5:
                source, step = rem(u + SIDE - 1 + 2 * turn, SIDE), SIDE + 1 - 2 * turn
            else:
                source = u
            block = g.at[i, source]
            uu, vv = rem(u + step, SIDE), v
        xx = vv * (1 - par) + uu * par
        yy = uu * (1 - par) + vv * par
        return pltpu.make_async_remote_copy(
            src_ref=block, dst_ref=block, send_sem=gs.at[i, k], recv_sem=gr.at[i, k],
            device_id=(dp, xx * SIDE + yy), device_id_type=MESH,
        )

    def stage_a(i):
        load_g(i, 0).wait()
        load_g(i, 1).wait()
        move(i, 0).start()
        move(i, 1).start()

    def stage_b(i):
        move(i, 0).wait_recv()
        move(i, 1).wait_recv()
        move(i, 2).start()

    def stage_c(i):
        move(i, 2).wait_recv()
        move(i, 3).start()
        move(i, 4).start()

    def stage_d(i):
        move(i, 3).wait_recv()
        move(i, 4).wait_recv()
        move(i, 5).start()

    def meta_copy(j):
        other = rem(me + j, OWNERS)
        return pltpu.make_async_remote_copy(
            src_ref=meta_out.at[other], dst_ref=meta_in.at[me], send_sem=ms.at[j], recv_sem=mr.at[j],
            device_id=(dp, other), device_id_type=MESH,
        )

    def prod_copy(j):
        other = rem(me + j, OWNERS)
        return pltpu.make_async_remote_copy(
            src_ref=prod_out.at[other], dst_ref=prod_in.at[me], send_sem=rs.at[j], recv_sem=rr.at[j],
            device_id=(dp, other), device_id_type=MESH,
        )

    def for_peers(act):
        def body(j, carry):
            act(j)
            return carry

        lax.fori_loop(1, OWNERS, body, 0)

    def gates(b, size):
        at = pl.ds(b * size, size)
        a = stored[at, :hid_n].astype(F32)
        up = stored[at, hid_n:].astype(F32)
        sg = jax.nn.sigmoid(a)
        act = a * sg
        hidden[at, :] = (act * up).astype(BF16)
        d_gate[at, :] = up * sg * (1.0 + a * (1.0 - sg))
        d_up[at, :] = act

    def build_pick():
        sub16 = lax.broadcasted_iota(jnp.int32, (HALF, HALF), 0)
        slot_rows = jnp.full((HALF, HALF), -1.0, F32)
        prob_rows = jnp.zeros((HALF, HALF), F32)
        for s in range(OWNERS):
            slot_rows = jnp.where(sub16 == s, jnp.broadcast_to(meta_in[s, 0:1, :], (HALF, HALF)), slot_rows)
            prob_rows = jnp.where(sub16 == s, jnp.broadcast_to(meta_in[s, 1:2, :], (HALF, HALF)), prob_rows)
        slot_cols = slot_rows.T
        prob_cols = prob_rows.T
        for par in range(2):
            for block in range(OWNERS):
                outer, inner = block // SIDE, block % SIDE
                s = inner * SIDE + outer if par == 0 else block
                col = slot_cols[0:tok, s : s + 1]
                place = jnp.where(col >= 0.0, col + float(cap * s), -1.0)
                cols[block * tok : (block + 1) * tok, :] = jnp.where(
                    lane == 0,
                    jnp.broadcast_to(place, (tok, HALF)),
                    jnp.broadcast_to(prob_cols[0:tok, s : s + 1], (tok, HALF)),
                )
            flat = cols[...].T
            place_row = flat[0:1, :].astype(jnp.int32)
            n_tok = OWNERS * tok
            match = jnp.broadcast_to(place_row, (rows, n_tok)) == lax.broadcasted_iota(jnp.int32, (rows, n_tok), 0)
            pick[par] = jnp.where(match, 1.0, 0.0).astype(BF16)
            if par == 0:
                total = jnp.sum(
                    jnp.where(match, jnp.broadcast_to(flat[1:2, :], (rows, n_tok)), 0.0), axis=1, keepdims=True
                )
                prob_col[...] = jnp.broadcast_to(total, (rows, HALF))

    def sib_copy(i):
        at = pl.ds(4 * i, 4)
        return pltpu.make_async_remote_copy(
            src_ref=part.at[at, 1 - core], dst_ref=part_in.at[at], send_sem=ss.at[i], recv_sem=sr.at[i],
            device_id=sibling, device_id_type=MESH,
        )

    def stage_e(i):
        move(i, 5).wait_recv()
        tokens = g[i].reshape(OWNERS * tok, WIDTH)
        routed = jnp.dot(pick[rem(i, 2)], tokens, preferred_element_type=F32)
        routed_all[i] = routed.astype(BF16)
        weight_row = jnp.concatenate([prob_col[...], prob_col[...]], axis=1)
        scaled = (weight_row * routed).astype(BF16)
        summed = lax.dot_general(
            scaled, hidden[...], (((0,), (0,)), ((), ())), preferred_element_type=F32
        )
        part[pl.ds(4 * i, 4)] = summed.astype(BF16).reshape(4, 2, SUBS, SHARE // SUBS, hid_n)
        sib_copy(i).start()

    def add_back(i):
        load_w(i, 0).wait()
        load_w(i, 1).wait()
        back[...] += jnp.dot(routed_all[i], w[i], preferred_element_type=F32)

    def chip_slot(off):
        at = off + STEPS
        m = rem(div(at, 2), n_groups)
        high = div(m, CHUNKS)
        chunk = (1 - high) * (7 - 2 * div(m, 2)) + high * 2 * div(m - CHUNKS * high, 2)
        return 4 * chunk + 2 * rem(m, 2) + rem(at, 2)

    def hop(way, s, k):
        return pltpu.make_async_remote_copy(
            src_ref=acc_out.at[way, s, k], dst_ref=acc_in.at[way, s + 1, k],
            send_sem=zs.at[way, s, k], recv_sem=zr.at[way, s, k],
            device_id=(up_z, down_z)[way], device_id_type=MESH,
        )

    def local_sum(slot, k):
        return part[slot, core, k].astype(F32) + part_in[slot, k].astype(F32)

    def ring_step(s, ways=(0, 1), first=None):
        for k in range(SUBS):
            for way in ways:
                slot = chip_slot(odd - s) if way == 0 else chip_slot(odd + 1 + s)

                def arrive():
                    hop(way, s - 1, k).wait_recv()

                if first is None:
                    pl.when(s > 0)(arrive)
                else:
                    arrive()
                acc_out[way, s, k] = (acc_in[way, s, k].astype(F32) + local_sum(slot, k)).astype(BF16)
                hop(way, s, k).start()

    for_peers(lambda j: meta_copy(j).start())
    stage_a(0)
    stage_a(1)
    load_stored.wait()
    quarter = rows // 4
    gates(0, quarter)
    stage_b(0)
    stage_b(1)
    stage_a(2)
    gates(1, quarter)
    stage_c(0)
    stage_c(1)
    stage_b(2)
    stage_a(3)
    for_peers(lambda j: meta_copy(j).wait_recv())
    build_pick()
    stage_d(0)
    stage_d(1)
    stage_c(2)
    stage_b(3)
    stage_a(4)
    gates(2, quarter)
    gates(3, quarter)
    back[...] = jnp.zeros_like(back)
    acc_in[0, 0] = jnp.zeros(acc_in.shape[2:], BF16)
    acc_in[1, 0] = jnp.zeros(acc_in.shape[2:], BF16)
    stage_d(2)
    stage_c(3)
    stage_b(4)
    stage_a(5)

    def pair(i, carry):
        stage_e(i)
        return carry

    lax.fori_loop(0, 2, pair, 0)
    sib_copy(0).wait_recv()

    def turn_body(j, carry):
        sib_copy(j + 1).wait_recv()
        ring_step(2 * j)

        @pl.when(j < 5)
        def _():
            stage_d(j + 3)

        @pl.when(j < 4)
        def _():
            stage_c(j + 4)

        @pl.when(j < 3)
        def _():
            stage_b(j + 5)

        @pl.when(j < 2)
        def _():
            stage_a(j + 6)

        stage_e(j + 2)
        ring_step(2 * j + 1)
        add_back(j)
        return carry

    lax.fori_loop(0, 6, turn_body, 0)
    sib_copy(7).wait_recv()
    ring_step(12, first=False)
    add_back(6)
    add_back(7)
    ring_step(13, first=False)

    products = jnp.sum(hidden[...].astype(F32) * back[...], axis=1, keepdims=True)
    row_at = lax.broadcasted_iota(jnp.int32, (rows, HALF), 0).astype(F32)
    row_slot = row_at - float(cap) * jnp.floor((row_at + 0.5) * (1.0 / cap))
    lane_at = lax.broadcasted_iota(jnp.int32, (rows, HALF), 1).astype(F32)
    spread = jnp.where(lane_at == row_slot, jnp.broadcast_to(products, (rows, HALF)), 0.0)
    src_at = jnp.floor((lax.broadcasted_iota(jnp.int32, (OWNERS, rows), 1).astype(F32) + 0.5) * (1.0 / cap))
    gather = jnp.where(src_at == lax.broadcasted_iota(jnp.int32, (OWNERS, rows), 0).astype(F32), 1.0, 0.0)
    by_source = jnp.dot(gather, spread, preferred_element_type=F32, precision=lax.Precision.HIGHEST)
    for s in range(OWNERS):
        prod_out[s] = jnp.broadcast_to(by_source[s : s + 1], (8, HALF))
    prod_in[me] = prod_out[me]
    for_peers(lambda j: prod_copy(j).start())

    ring_step(14, first=False)

    def finish_rows(b, size):
        at = pl.ds(b * size, size)
        scale = jnp.concatenate([prob_col[at, :]] * (hid_n // HALF), axis=1)
        grad = scale * back[at, :]
        pre[at, :hid_n] = (grad * d_gate[at, :]).astype(BF16)
        pre[at, hid_n:] = (grad * d_up[at, :]).astype(BF16)

    def store_pre(b, size):
        at = pl.ds(b * size, size)
        return pltpu.make_async_copy(pre.at[at], pre_hbm.at[at], sem_pre.at[b])

    half_rows = rows // 2
    finish_rows(0, half_rows)
    store_pre(0, half_rows).start()
    ring_step(15, ways=(0,), first=False)
    finish_rows(1, half_rows)
    store_pre(1, half_rows).start()

    for_peers(lambda j: prod_copy(j).wait_recv())
    lane_f = lane.astype(F32)
    per_owner = jnp.zeros((tok, HALF), F32)
    for e in range(OWNERS):
        hit = jnp.broadcast_to(slot_tab[:, e : e + 1], (tok, HALF)) == lane_f
        value = jnp.sum(
            jnp.where(hit, jnp.broadcast_to(prod_in[e, 0:1, :], (tok, HALF)), 0.0), axis=1, keepdims=True
        )
        per_owner = jnp.where(lane == e, jnp.broadcast_to(value, (tok, HALF)), per_owner)
    lane_top = lax.broadcasted_iota(jnp.int32, (tok, top), 1)
    result = jnp.zeros((tok, top), F32)
    for k in range(top):
        value = jnp.sum(jnp.where(ids_ref[:, k : k + 1] == lane, per_owner, 0.0), axis=1, keepdims=True)
        result = jnp.where(lane_top == k, jnp.broadcast_to(value, (tok, top)), result)
    gprobs_ref[...] = result

    own = chip_slot(odd - STEPS)
    piece = SHARE // SUBS
    for k in range(SUBS):
        hop(1, STEPS - 2, k).wait_recv()
        hop(0, STEPS - 1, k).wait_recv()
        down_ref[0, k * piece : (k + 1) * piece, :] = (
            acc_in[0, STEPS, k].astype(F32) + acc_in[1, STEPS - 1, k].astype(F32) + local_sum(own, k)
        )

    def drain(i, carry):
        for k in range(6):
            move(i, k).wait_send()
        sib_copy(i).wait_send()
        return carry

    lax.fori_loop(0, CHUNKS, drain, 0)
    for_peers(lambda j: meta_copy(j).wait_send())
    for_peers(lambda j: prod_copy(j).wait_send())

    def drain_ring(s, carry):
        for k in range(SUBS):
            for way in range(2):
                hop(way, s, k).wait_send()
        return carry

    lax.fori_loop(0, STEPS - 1, drain_ring, 0)
    for k in range(SUBS):
        hop(0, STEPS - 1, k).wait_send()
    store_pre(0, half_rows).wait()
    store_pre(1, half_rows).wait()


def local(out_grad, probs, expert_ids, saved_pre, down_weight):
    tok, top = expert_ids.shape
    rows, pre_n = saved_pre.shape
    hid_n = pre_n // 2
    piece = SHARE // SUBS
    dma = pltpu.SemaphoreType.DMA
    scratch = [
        pltpu.VMEM((CHUNKS, SIDE, SIDE, tok, WIDTH), BF16),
        pltpu.VMEM((CHUNKS, WIDTH, hid_n), BF16),
        pltpu.VMEM((rows, pre_n), BF16),
        pltpu.VMEM((rows, hid_n), BF16),
        pltpu.VMEM((rows, hid_n), F32),
        pltpu.VMEM((rows, hid_n), F32),
        pltpu.VMEM((rows, hid_n), F32),
        pltpu.VMEM((CHUNKS, rows, WIDTH), BF16),
        pltpu.VMEM((rows, pre_n), BF16),
        pltpu.VMEM((2, rows, OWNERS * tok), BF16),
        pltpu.VMEM((rows, HALF), F32),
        pltpu.VMEM((OWNERS * tok, HALF), F32),
        pltpu.VMEM((tok, HALF), F32),
        pltpu.VMEM((OWNERS, 8, HALF), F32),
        pltpu.VMEM((OWNERS, 8, HALF), F32),
        pltpu.VMEM((OWNERS, 8, HALF), F32),
        pltpu.VMEM((OWNERS, 8, HALF), F32),
        pltpu.VMEM((CHIPS, 2, SUBS, piece, hid_n), BF16),
        pltpu.VMEM((CHIPS, SUBS, piece, hid_n), BF16),
        pltpu.VMEM((2, STEPS, SUBS, piece, hid_n), BF16),
        pltpu.VMEM((2, STEPS + 1, SUBS, piece, hid_n), BF16),
        dma((CHUNKS, 2)), dma((CHUNKS, 2)), dma, dma((2,)),
        dma((CHUNKS, 6)), dma((CHUNKS, 6)),
        dma((OWNERS,)), dma((OWNERS,)), dma((OWNERS,)), dma((OWNERS,)),
        dma((CHUNKS,)), dma((CHUNKS,)),
        dma((2, STEPS, SUBS)), dma((2, STEPS, SUBS)),
    ]
    hbm = pl.BlockSpec(memory_space=pl.ANY)
    vmem = pl.BlockSpec(memory_space=pltpu.VMEM)
    return pl.pallas_call(
        kernel,
        out_shape=(
            jax.ShapeDtypeStruct((1, SHARE, hid_n), F32),
            jax.ShapeDtypeStruct((rows, pre_n), BF16),
            jax.ShapeDtypeStruct((tok, top), F32),
        ),
        in_specs=[hbm, vmem, vmem, hbm, hbm],
        out_specs=(vmem, hbm, vmem),
        scratch_shapes=scratch,
        compiler_params=pltpu.CompilerParams(
            collective_id=0, has_side_effects=True, vmem_limit_bytes=56 * 1024 * 1024
        ),
    )(out_grad, probs, expert_ids, saved_pre, down_weight)


def solution(mesh):
    in_specs = (
        P(("dp", "expert"), None),
        P(("dp", "expert"), None),
        P(("dp", "expert"), None),
        P(("dp", "expert"), None),
        P("expert", None, None),
    )
    out_specs = (P("expert", "dp", None), P(("dp", "expert"), None), P(("dp", "expert"), None))
    return jax.shard_map(local, mesh=mesh, in_specs=in_specs, out_specs=out_specs, check_vma=False)
```

```python
import jax
import jax.numpy as jnp
from jax import lax
from jax.experimental import pallas as pl
from jax.experimental.pallas import tpu as pltpu
from jax.sharding import PartitionSpec as P

MESH = pl.DeviceIdType.MESH
F32, BF16 = jnp.float32, jnp.bfloat16
PAD = 32
OWNERS = 16
CHUNKS = 8
WIDTH = 256
HALF = 128
REACH = 16
STEPS = 8
CHIPS = 32
SHARE = 32
SUBS = 2


def div(a, b):
    return lax.div(jnp.int32(a), jnp.int32(b))


def rem(a, b):
    return lax.rem(jnp.int32(a), jnp.int32(b))


def kernel(
    grad_hbm, probs_ref, ids_ref, stored_hbm, weight_hbm,
    down_ref, pre_hbm, gprobs_ref,
    own_g, w, stored, hidden, d_gate, d_up, back, routed_all, pre,
    select, rows_out, rows_in, prob_out, prob_in, compact, prob_col,
    prod_out, prod_in, part, part_in, acc_out, acc_in, leaf_out, leaf_in,
    sem_g, sem_w, sem_stored, sem_pre, gs, gr, ps, pr, rs, rr, ss, sr, zs, zr, ls, lr,
):
    top, tok = ids_ref.shape
    rows = stored_hbm.shape[0]
    hid_n = weight_hbm.shape[2]
    cap = rows // OWNERS
    dp = lax.axis_index("dp")
    me = lax.axis_index("expert")
    z, core = div(dp, 2), rem(dp, 2)
    odd = rem(z, 2)
    first_group = div(z + REACH, 2)
    n_groups = 2 * CHUNKS
    near = [(rem(z + by, CHIPS) * 2 + core, me) for by in (1, CHIPS - 1)]
    far = [(rem(z + by, CHIPS) * 2 + core, me) for by in (2, CHIPS - 2)]
    sibling = (z * 2 + 1 - core, me)

    barrier = pltpu.get_barrier_semaphore()

    def greet(j, carry):
        pl.semaphore_signal(barrier, inc=1, device_id=(dp, rem(me + j, OWNERS)), device_id_type=MESH)
        return carry

    for target in (*near, *far, sibling):
        pl.semaphore_signal(barrier, inc=1, device_id=target, device_id_type=MESH)
    lax.fori_loop(1, OWNERS, greet, 0)

    def group_of(i, half):
        par = rem(i, 2)
        start = (1 - par) * i - par * (i + 1)
        return rem(first_group + start + half + 2 * n_groups, n_groups)

    def load_g(i, half):
        at = pl.multiple_of(group_of(i, half) * HALF, HALF)
        return pltpu.make_async_copy(
            grad_hbm.at[:, pl.ds(at, HALF)], own_g.at[i, :, pl.ds(half * HALF, HALF)], sem_g.at[i, half]
        )

    def load_w(i, half):
        at = pl.multiple_of(group_of(i, half) * HALF, HALF)
        return pltpu.make_async_copy(
            weight_hbm.at[0, pl.ds(at, HALF), :], w.at[i, pl.ds(half * HALF, HALF), :], sem_w.at[i, half]
        )

    for i in range(CHUNKS):
        for half in range(2):
            load_g(i, half).start()
    load_stored = pltpu.make_async_copy(stored_hbm, stored, sem_stored)
    load_stored.start()
    for i in range(CHUNKS):
        for half in range(2):
            load_w(i, half).start()

    ids = ids_ref[...]
    owner = lax.broadcasted_iota(jnp.int32, (OWNERS, tok), 0)
    chosen = jnp.zeros((OWNERS, tok), F32)
    prob = jnp.zeros((OWNERS, tok), F32)
    probs = probs_ref[...].astype(F32)
    for k in range(top):
        hit = jnp.broadcast_to(ids[k : k + 1], (OWNERS, tok)) == owner
        chosen = chosen + jnp.where(hit, 1.0, 0.0)
        prob = prob + jnp.where(hit, jnp.broadcast_to(probs[k : k + 1], (OWNERS, tok)), 0.0)
    earlier = (
        lax.broadcasted_iota(jnp.int32, (tok, tok), 0) < lax.broadcasted_iota(jnp.int32, (tok, tok), 1)
    )
    before = jnp.dot(
        chosen.astype(BF16), jnp.where(earlier, 1.0, 0.0).astype(BF16), preferred_element_type=F32
    )
    slots = jnp.where(chosen > 0.0, before, -1.0)
    slot_at = lax.broadcasted_iota(jnp.int32, (PAD, tok), 0).astype(F32)
    for e in range(OWNERS):
        match = jnp.broadcast_to(slots[e : e + 1], (PAD, tok)) == slot_at
        select[e * PAD : (e + 1) * PAD, :] = jnp.where(match, 1.0, 0.0).astype(BF16)
        filled = jnp.sum(
            jnp.where(match, jnp.broadcast_to(prob[e : e + 1], (PAD, tok)), 0.0), axis=1, keepdims=True
        )
        prob_out[e] = jnp.broadcast_to(filled, (PAD, HALF)).astype(BF16)

    def pick_rows(i):
        load_g(i, 0).wait()
        load_g(i, 1).wait()
        picked = jnp.dot(select[...], own_g[i], preferred_element_type=F32)
        rows_out[i] = picked.astype(BF16).reshape(OWNERS, PAD, WIDTH)
        rows_in[i, me] = rows_out[i, me]

    pick_rows(0)
    prob_in[me] = prob_out[me]
    pl.semaphore_wait(barrier, OWNERS - 1 + 5)

    def row_copy(i, j):
        other = rem(me + j, OWNERS)
        return pltpu.make_async_remote_copy(
            src_ref=rows_out.at[i, other], dst_ref=rows_in.at[i, me], send_sem=gs.at[i, j], recv_sem=gr.at[i, j],
            device_id=(dp, other), device_id_type=MESH,
        )

    def prob_copy(j):
        other = rem(me + j, OWNERS)
        return pltpu.make_async_remote_copy(
            src_ref=prob_out.at[other], dst_ref=prob_in.at[me], send_sem=ps.at[j], recv_sem=pr.at[j],
            device_id=(dp, other), device_id_type=MESH,
        )

    def prod_copy(j):
        other = rem(me + j, OWNERS)
        return pltpu.make_async_remote_copy(
            src_ref=prod_out.at[other], dst_ref=prod_in.at[me], send_sem=rs.at[j], recv_sem=rr.at[j],
            device_id=(dp, other), device_id_type=MESH,
        )

    def for_peers(act):
        def body(j, carry):
            act(j)
            return carry

        lax.fori_loop(1, OWNERS, body, 0)

    def send_rows(i):
        for_peers(lambda j: row_copy(i, j).start())

    def gates(b, size):
        at = pl.ds(b * size, size)
        a = stored[at, :hid_n].astype(F32)
        up = stored[at, hid_n:].astype(F32)
        sg = jax.nn.sigmoid(a)
        act = a * sg
        hidden[at, :] = (act * up).astype(BF16)
        d_gate[at, :] = up * sg * (1.0 + a * (1.0 - sg))
        d_up[at, :] = act

    def sib_copy(i):
        at = pl.ds(4 * i, 4)
        return pltpu.make_async_remote_copy(
            src_ref=part.at[at, 1 - core], dst_ref=part_in.at[at], send_sem=ss.at[i], recv_sem=sr.at[i],
            device_id=sibling, device_id_type=MESH,
        )

    def stage_e(i):
        for_peers(lambda j: row_copy(i, j).wait_recv())
        arrived = rows_in[i].reshape(OWNERS * PAD, WIDTH)
        routed = jnp.dot(compact[...], arrived, preferred_element_type=F32)
        routed_all[i] = routed.astype(BF16)
        weight_row = jnp.concatenate([prob_col[...], prob_col[...]], axis=1)
        scaled = (weight_row * routed).astype(BF16)
        summed = lax.dot_general(
            scaled, hidden[...], (((0,), (0,)), ((), ())), preferred_element_type=F32
        )
        part[pl.ds(4 * i, 4)] = summed.astype(BF16).reshape(4, 2, SUBS, SHARE // SUBS, hid_n)
        sib_copy(i).start()

    def add_back(i):
        load_w(i, 0).wait()
        load_w(i, 1).wait()
        back[...] += jnp.dot(routed_all[i], w[i], preferred_element_type=F32)

    def chip_slot(off):
        at = off + REACH
        m = rem(div(at, 2), n_groups)
        high = div(m, CHUNKS)
        chunk = (1 - high) * (7 - 2 * div(m, 2)) + high * 2 * div(m - CHUNKS * high, 2)
        return 4 * chunk + 2 * rem(m, 2) + rem(at, 2)

    def hop(way, t, k):
        return pltpu.make_async_remote_copy(
            src_ref=acc_out.at[way, t, k], dst_ref=acc_in.at[way, t + 1, k],
            send_sem=zs.at[way, t, k], recv_sem=zr.at[way, t, k],
            device_id=far[way], device_id_type=MESH,
        )

    def leaf(way, t):
        return pltpu.make_async_remote_copy(
            src_ref=leaf_out.at[way, t], dst_ref=leaf_in.at[way, t + 1],
            send_sem=ls.at[way, t], recv_sem=lr.at[way, t],
            device_id=near[way], device_id_type=MESH,
        )

    def local_sum(slot, k):
        return part[slot, core, k].astype(F32) + part_in[slot, k].astype(F32)

    def guarded(condition, act):
        if isinstance(condition, bool):
            if condition:
                act()
        else:
            pl.when(condition)(act)

    def ring_step(t):
        for way in range(2):
            slot = chip_slot(odd - 2 * t - 1) if way == 0 else chip_slot(odd + 1 + 2 * t)
            for k in range(SUBS):
                leaf_out[way, t, k] = local_sum(slot, k).astype(BF16)
            leaf(way, t).start()

        def pass_on(way, k, slot):
            if k == 0:
                guarded(t > 0, lambda: leaf(way, t - 1).wait_recv())
            guarded(t > way, lambda: hop(way, t - 1, k).wait_recv())
            acc_out[way, t, k] = (
                acc_in[way, t, k].astype(F32) + leaf_in[way, t, k].astype(F32) + local_sum(slot, k)
            ).astype(BF16)
            hop(way, t, k).start()

        for k in range(SUBS):
            pass_on(0, k, chip_slot(odd - 2 * t))
            guarded(t > 0, lambda: pass_on(1, k, chip_slot(odd + 2 * t)))

    send_rows(0)
    for_peers(lambda j: prob_copy(j).start())
    pick_rows(1)
    send_rows(1)
    load_stored.wait()
    quarter = rows // 4
    gates(0, quarter)
    gates(1, quarter)
    pick_rows(2)
    send_rows(2)
    gates(2, quarter)
    gates(3, quarter)
    pick_rows(3)
    pick_rows(4)
    row_at = lax.broadcasted_iota(jnp.int32, (rows, OWNERS * PAD), 0).astype(F32)
    padded_at = row_at + float(PAD - cap) * jnp.floor((row_at + 0.5) * (1.0 / cap))
    compact[...] = jnp.where(
        lax.broadcasted_iota(jnp.int32, (rows, OWNERS * PAD), 1).astype(F32) == padded_at, 1.0, 0.0
    ).astype(BF16)
    acc_in[0, 0] = jnp.zeros(acc_in.shape[2:], BF16)
    acc_in[1, 1] = jnp.zeros(acc_in.shape[2:], BF16)
    leaf_in[0, 0] = jnp.zeros(leaf_in.shape[2:], BF16)
    send_rows(3)
    for_peers(lambda j: prob_copy(j).wait_recv())
    prob_col[...] = jnp.dot(
        compact[...], prob_in[...].reshape(OWNERS * PAD, HALF), preferred_element_type=F32
    )
    back[...] = jnp.zeros_like(back)

    def early(i, carry):
        stage_e(i)
        return carry

    lax.fori_loop(0, 3, early, 0)
    send_rows(4)
    sib_copy(0).wait_recv()

    def turn(t, carry):
        sib_copy(t + 1).wait_recv()
        ring_step(t)

        @pl.when(t < 3)
        def _():
            pick_rows(t + 5)
            send_rows(t + 5)

        @pl.when(t < 5)
        def _():
            stage_e(t + 3)

        add_back(t)
        return carry

    lax.fori_loop(0, 6, turn, 0)
    add_back(6)
    sib_copy(7).wait_recv()
    ring_step(6)
    add_back(7)

    products = jnp.sum(hidden[...].astype(F32) * back[...], axis=1, keepdims=True)
    row_at = lax.broadcasted_iota(jnp.int32, (rows, HALF), 0).astype(F32)
    row_slot = row_at - float(cap) * jnp.floor((row_at + 0.5) * (1.0 / cap))
    lane_at = lax.broadcasted_iota(jnp.int32, (rows, HALF), 1).astype(F32)
    spread = jnp.where(lane_at == row_slot, jnp.broadcast_to(products, (rows, HALF)), 0.0)
    src_at = jnp.floor((lax.broadcasted_iota(jnp.int32, (OWNERS, rows), 1).astype(F32) + 0.5) * (1.0 / cap))
    gather = jnp.where(src_at == lax.broadcasted_iota(jnp.int32, (OWNERS, rows), 0).astype(F32), 1.0, 0.0)
    by_source = jnp.dot(gather, spread, preferred_element_type=F32, precision=lax.Precision.HIGHEST)
    for s in range(OWNERS):
        prod_out[s] = jnp.broadcast_to(by_source[s : s + 1], (8, HALF))
    prod_in[me] = prod_out[me]
    for_peers(lambda j: prod_copy(j).start())

    def finish_rows(b, size):
        at = pl.ds(b * size, size)
        scale = jnp.concatenate([prob_col[at, :]] * (hid_n // HALF), axis=1)
        grad = scale * back[at, :]
        pre[at, :hid_n] = (grad * d_gate[at, :]).astype(BF16)
        pre[at, hid_n:] = (grad * d_up[at, :]).astype(BF16)

    def store_pre(b, size):
        at = pl.ds(b * size, size)
        return pltpu.make_async_copy(pre.at[at], pre_hbm.at[at], sem_pre.at[b])

    half_rows = rows // 2
    finish_rows(0, half_rows)
    store_pre(0, half_rows).start()
    ring_step(7)
    finish_rows(1, half_rows)
    store_pre(1, half_rows).start()

    for_peers(lambda j: prod_copy(j).wait_recv())
    sub16 = lax.broadcasted_iota(jnp.int32, (OWNERS, HALF), 0)
    by_owner = jnp.zeros((OWNERS, HALF), F32)
    for e in range(OWNERS):
        by_owner = jnp.where(sub16 == e, jnp.broadcast_to(prod_in[e, 0:1, :], (OWNERS, HALF)), by_owner)
    by_slot = jnp.concatenate([by_owner, jnp.zeros((HALF - OWNERS, HALF), F32)], axis=0).T
    result = jnp.zeros((top, tok), F32)
    for e in range(OWNERS):
        match = jnp.broadcast_to(slots[e : e + 1], (PAD, tok)) == slot_at
        value = jnp.sum(
            jnp.where(match, jnp.broadcast_to(by_slot[0:PAD, e : e + 1], (PAD, tok)), 0.0), axis=0, keepdims=True
        )
        result = jnp.where(ids == e, jnp.broadcast_to(value, (top, tok)), result)
    gprobs_ref[...] = result

    def drain(i, carry):
        for_peers(lambda j: row_copy(i, j).wait_send())
        sib_copy(i).wait_send()
        return carry

    lax.fori_loop(0, CHUNKS, drain, 0)
    for_peers(lambda j: prob_copy(j).wait_send())
    for_peers(lambda j: prod_copy(j).wait_send())
    for way in range(2):

        def drain_ring(t, carry):
            for k in range(SUBS):
                hop(way, t, k).wait_send()
            return carry

        def drain_leaf(t, carry):
            leaf(way, t).wait_send()
            return carry

        lax.fori_loop(way, STEPS - 1, drain_ring, 0)
        lax.fori_loop(0, STEPS - 1, drain_leaf, 0)

    own = chip_slot(odd - REACH)
    piece = SHARE // SUBS
    for way in range(2):
        leaf(way, STEPS - 1).wait_recv()
    for k in range(SUBS):
        for way in range(2):
            hop(way, STEPS - 1, k).wait_recv()
        down_ref[0, k * piece : (k + 1) * piece, :] = (
            (acc_in[0, STEPS, k].astype(F32) + acc_in[1, STEPS, k].astype(F32))
            + (leaf_in[0, STEPS, k].astype(F32) + leaf_in[1, STEPS, k].astype(F32))
            + local_sum(own, k)
        )

    for way in range(2):
        leaf(way, STEPS - 1).wait_send()
        for k in range(SUBS):
            hop(way, STEPS - 1, k).wait_send()
    store_pre(0, half_rows).wait()
    store_pre(1, half_rows).wait()


def local(out_grad, probs, expert_ids, saved_pre, down_weight):
    top, tok = expert_ids.shape[1], expert_ids.shape[0]
    rows, pre_n = saved_pre.shape
    hid_n = pre_n // 2
    piece = SHARE // SUBS
    dma = pltpu.SemaphoreType.DMA
    scratch = [
        pltpu.VMEM((CHUNKS, tok, WIDTH), BF16),
        pltpu.VMEM((CHUNKS, WIDTH, hid_n), BF16),
        pltpu.VMEM((rows, pre_n), BF16),
        pltpu.VMEM((rows, hid_n), BF16),
        pltpu.VMEM((rows, hid_n), F32),
        pltpu.VMEM((rows, hid_n), F32),
        pltpu.VMEM((rows, hid_n), F32),
        pltpu.VMEM((CHUNKS, rows, WIDTH), BF16),
        pltpu.VMEM((rows, pre_n), BF16),
        pltpu.VMEM((OWNERS * PAD, tok), BF16),
        pltpu.VMEM((CHUNKS, OWNERS, PAD, WIDTH), BF16),
        pltpu.VMEM((CHUNKS, OWNERS, PAD, WIDTH), BF16),
        pltpu.VMEM((OWNERS, PAD, HALF), BF16),
        pltpu.VMEM((OWNERS, PAD, HALF), BF16),
        pltpu.VMEM((rows, OWNERS * PAD), BF16),
        pltpu.VMEM((rows, HALF), F32),
        pltpu.VMEM((OWNERS, 8, HALF), F32),
        pltpu.VMEM((OWNERS, 8, HALF), F32),
        pltpu.VMEM((CHIPS, 2, SUBS, piece, hid_n), BF16),
        pltpu.VMEM((CHIPS, SUBS, piece, hid_n), BF16),
        pltpu.VMEM((2, STEPS, SUBS, piece, hid_n), BF16),
        pltpu.VMEM((2, STEPS + 1, SUBS, piece, hid_n), BF16),
        pltpu.VMEM((2, STEPS, SUBS, piece, hid_n), BF16),
        pltpu.VMEM((2, STEPS + 1, SUBS, piece, hid_n), BF16),
        dma((CHUNKS, 2)), dma((CHUNKS, 2)), dma, dma((2,)),
        dma((CHUNKS, OWNERS)), dma((CHUNKS, OWNERS)),
        dma((OWNERS,)), dma((OWNERS,)), dma((OWNERS,)), dma((OWNERS,)),
        dma((CHUNKS,)), dma((CHUNKS,)),
        dma((2, STEPS, SUBS)), dma((2, STEPS, SUBS)), dma((2, STEPS)), dma((2, STEPS)),
    ]
    hbm = pl.BlockSpec(memory_space=pl.ANY)
    vmem = pl.BlockSpec(memory_space=pltpu.VMEM)
    down, pre, gprobs = pl.pallas_call(
        kernel,
        out_shape=(
            jax.ShapeDtypeStruct((1, SHARE, hid_n), F32),
            jax.ShapeDtypeStruct((rows, pre_n), BF16),
            jax.ShapeDtypeStruct((top, tok), F32),
        ),
        in_specs=[hbm, vmem, vmem, hbm, hbm],
        out_specs=(vmem, hbm, vmem),
        scratch_shapes=scratch,
        compiler_params=pltpu.CompilerParams(
            collective_id=0, has_side_effects=True, vmem_limit_bytes=56 * 1024 * 1024
        ),
    )(out_grad, probs.T, expert_ids.T, saved_pre, down_weight)
    return down, pre, gprobs.T


def solution(mesh):
    in_specs = (
        P(("dp", "expert"), None),
        P(("dp", "expert"), None),
        P(("dp", "expert"), None),
        P(("dp", "expert"), None),
        P("expert", None, None),
    )
    out_specs = (P("expert", "dp", None), P(("dp", "expert"), None), P(("dp", "expert"), None))
    return jax.shard_map(local, mesh=mesh, in_specs=in_specs, out_specs=out_specs, check_vma=False)
```

```python
import jax
import jax.numpy as jnp
from jax import lax
from jax.experimental import pallas as pl
from jax.experimental.pallas import tpu as pltpu
from jax.sharding import PartitionSpec as P

MESH = pl.DeviceIdType.MESH
F32, BF16 = jnp.float32, jnp.bfloat16
PAD = 32
OWNERS = 16
CHUNKS = 8
WIDTH = 256
HALF = 128
REACH = 16
STEPS = 8
CHIPS = 32
SHARE = 32
SUBS = 2


def div(a, b):
    return lax.div(jnp.int32(a), jnp.int32(b))


def rem(a, b):
    return lax.rem(jnp.int32(a), jnp.int32(b))


def kernel(
    grad_hbm, probs_ref, ids_ref, stored_hbm, weight_hbm,
    down_ref, pre_hbm, gprobs_ref,
    own_g, w, stored, hidden, d_gate, d_up, back, routed_all, pre,
    select, rows_out, rows_in, prob_out, prob_in, compact, prob_col,
    prod_out, prod_in, part, part_in, acc_out, acc_in, leaf_out, leaf_in,
    sem_g, sem_w, sem_stored, sem_pre, gs, gr, ps, pr, rs, rr, ss, sr, zs, zr, ls, lr,
):
    top, tok = ids_ref.shape
    rows = stored_hbm.shape[0]
    hid_n = weight_hbm.shape[2]
    cap = rows // OWNERS
    dp = lax.axis_index("dp")
    me = lax.axis_index("expert")
    z, core = div(dp, 2), rem(dp, 2)
    odd = rem(z, 2)
    first_group = div(z + REACH, 2)
    n_groups = 2 * CHUNKS
    near = [(rem(z + by, CHIPS) * 2 + core, me) for by in (1, CHIPS - 1)]
    far = [(rem(z + by, CHIPS) * 2 + core, me) for by in (2, CHIPS - 2)]
    sibling = (z * 2 + 1 - core, me)

    barrier = pltpu.get_barrier_semaphore()

    def greet(j, carry):
        pl.semaphore_signal(barrier, inc=1, device_id=(dp, rem(me + j, OWNERS)), device_id_type=MESH)
        return carry

    for target in (*near, *far, sibling):
        pl.semaphore_signal(barrier, inc=1, device_id=target, device_id_type=MESH)
    lax.fori_loop(1, OWNERS, greet, 0)

    def group_of(i, half):
        par = rem(i, 2)
        start = (1 - par) * i - par * (i + 1)
        return rem(first_group + start + half + 2 * n_groups, n_groups)

    def load_g(i, half):
        at = pl.multiple_of(group_of(i, half) * HALF, HALF)
        return pltpu.make_async_copy(
            grad_hbm.at[:, pl.ds(at, HALF)], own_g.at[i, :, pl.ds(half * HALF, HALF)], sem_g.at[i, half]
        )

    def load_w(i, half):
        at = pl.multiple_of(group_of(i, half) * HALF, HALF)
        return pltpu.make_async_copy(
            weight_hbm.at[0, pl.ds(at, HALF), :], w.at[i, pl.ds(half * HALF, HALF), :], sem_w.at[i, half]
        )

    for i in range(CHUNKS):
        for half in range(2):
            load_g(i, half).start()
    load_stored = pltpu.make_async_copy(stored_hbm, stored, sem_stored)
    load_stored.start()
    for i in range(CHUNKS):
        for half in range(2):
            load_w(i, half).start()

    ids = ids_ref[...]
    owner = lax.broadcasted_iota(jnp.int32, (OWNERS, tok), 0)
    chosen = jnp.zeros((OWNERS, tok), F32)
    prob = jnp.zeros((OWNERS, tok), F32)
    probs = probs_ref[...].astype(F32)
    for k in range(top):
        hit = jnp.broadcast_to(ids[k : k + 1], (OWNERS, tok)) == owner
        chosen = chosen + jnp.where(hit, 1.0, 0.0)
        prob = prob + jnp.where(hit, jnp.broadcast_to(probs[k : k + 1], (OWNERS, tok)), 0.0)
    earlier = (
        lax.broadcasted_iota(jnp.int32, (tok, tok), 0) < lax.broadcasted_iota(jnp.int32, (tok, tok), 1)
    )
    before = jnp.dot(
        chosen.astype(BF16), jnp.where(earlier, 1.0, 0.0).astype(BF16), preferred_element_type=F32
    )
    slots = jnp.where(chosen > 0.0, before, -1.0)
    slot_at = lax.broadcasted_iota(jnp.int32, (PAD, tok), 0).astype(F32)
    for e in range(OWNERS):
        match = jnp.broadcast_to(slots[e : e + 1], (PAD, tok)) == slot_at
        select[e * PAD : (e + 1) * PAD, :] = jnp.where(match, 1.0, 0.0).astype(BF16)
        filled = jnp.sum(
            jnp.where(match, jnp.broadcast_to(prob[e : e + 1], (PAD, tok)), 0.0), axis=1, keepdims=True
        )
        prob_out[e] = jnp.broadcast_to(filled, (PAD, HALF)).astype(BF16)

    def pick_rows(i):
        load_g(i, 0).wait()
        load_g(i, 1).wait()
        picked = jnp.dot(select[...], own_g[i], preferred_element_type=F32)
        rows_out[i] = picked.astype(BF16).reshape(OWNERS, PAD, WIDTH)
        rows_in[i, me] = rows_out[i, me]

    pick_rows(0)
    prob_in[me] = prob_out[me]
    pl.semaphore_wait(barrier, OWNERS - 1 + 5)

    def row_copy(i, j):
        other = rem(me + j, OWNERS)
        return pltpu.make_async_remote_copy(
            src_ref=rows_out.at[i, other], dst_ref=rows_in.at[i, me], send_sem=gs.at[i, j], recv_sem=gr.at[i, j],
            device_id=(dp, other), device_id_type=MESH,
        )

    def prob_copy(j):
        other = rem(me + j, OWNERS)
        return pltpu.make_async_remote_copy(
            src_ref=prob_out.at[other], dst_ref=prob_in.at[me], send_sem=ps.at[j], recv_sem=pr.at[j],
            device_id=(dp, other), device_id_type=MESH,
        )

    def prod_copy(j):
        other = rem(me + j, OWNERS)
        return pltpu.make_async_remote_copy(
            src_ref=prod_out.at[other], dst_ref=prod_in.at[me], send_sem=rs.at[j], recv_sem=rr.at[j],
            device_id=(dp, other), device_id_type=MESH,
        )

    def for_peers(act):
        def body(j, carry):
            act(j)
            return carry

        lax.fori_loop(1, OWNERS, body, 0)

    def send_rows(i):
        for_peers(lambda j: row_copy(i, j).start())

    def gates(b, size):
        at = pl.ds(b * size, size)
        a = stored[at, :hid_n].astype(F32)
        up = stored[at, hid_n:].astype(F32)
        sg = jax.nn.sigmoid(a)
        act = a * sg
        hidden[at, :] = (act * up).astype(BF16)
        d_gate[at, :] = up * sg * (1.0 + a * (1.0 - sg))
        d_up[at, :] = act

    def sib_copy(i):
        at = pl.ds(4 * i, 4)
        return pltpu.make_async_remote_copy(
            src_ref=part.at[at, 1 - core], dst_ref=part_in.at[at], send_sem=ss.at[i], recv_sem=sr.at[i],
            device_id=sibling, device_id_type=MESH,
        )

    def stage_e(i):
        for_peers(lambda j: row_copy(i, j).wait_recv())
        arrived = rows_in[i].reshape(OWNERS * PAD, WIDTH)
        routed = jnp.dot(compact[...], arrived, preferred_element_type=F32)
        routed_all[i] = routed.astype(BF16)
        weight_row = jnp.concatenate([prob_col[...], prob_col[...]], axis=1)
        scaled = (weight_row * routed).astype(BF16)
        summed = lax.dot_general(
            scaled, hidden[...], (((0,), (0,)), ((), ())), preferred_element_type=F32
        )
        part[pl.ds(4 * i, 4)] = summed.astype(BF16).reshape(4, 2, SUBS, SHARE // SUBS, hid_n)
        sib_copy(i).start()

    def add_back(i):
        load_w(i, 0).wait()
        load_w(i, 1).wait()
        back[...] += jnp.dot(routed_all[i], w[i], preferred_element_type=F32)

    def chip_slot(off):
        at = off + REACH
        m = rem(div(at, 2), n_groups)
        high = div(m, CHUNKS)
        chunk = (1 - high) * (7 - 2 * div(m, 2)) + high * 2 * div(m - CHUNKS * high, 2)
        return 4 * chunk + 2 * rem(m, 2) + rem(at, 2)

    def hop(way, t, k):
        return pltpu.make_async_remote_copy(
            src_ref=acc_out.at[way, t, k], dst_ref=acc_in.at[way, t + 1, k],
            send_sem=zs.at[way, t, k], recv_sem=zr.at[way, t, k],
            device_id=far[way], device_id_type=MESH,
        )

    def leaf(way, t):
        return pltpu.make_async_remote_copy(
            src_ref=leaf_out.at[way, t], dst_ref=leaf_in.at[way, t + 1],
            send_sem=ls.at[way, t], recv_sem=lr.at[way, t],
            device_id=near[way], device_id_type=MESH,
        )

    def local_sum(slot, k):
        return part[slot, core, k].astype(F32) + part_in[slot, k].astype(F32)

    def guarded(condition, act):
        if isinstance(condition, bool):
            if condition:
                act()
        else:
            pl.when(condition)(act)

    def ring_step(t):
        for way in range(2):
            slot = chip_slot(odd - 2 * t - 1) if way == 0 else chip_slot(odd + 1 + 2 * t)
            for k in range(SUBS):
                leaf_out[way, t, k] = local_sum(slot, k).astype(BF16)
            leaf(way, t).start()

        def pass_on(way, k, slot):
            if k == 0:
                guarded(t > 0, lambda: leaf(way, t - 1).wait_recv())
            guarded(t > way, lambda: hop(way, t - 1, k).wait_recv())
            acc_out[way, t, k] = (
                acc_in[way, t, k].astype(F32) + leaf_in[way, t, k].astype(F32) + local_sum(slot, k)
            ).astype(BF16)
            hop(way, t, k).start()

        for k in range(SUBS):
            pass_on(0, k, chip_slot(odd - 2 * t))
            guarded(t > 0, lambda: pass_on(1, k, chip_slot(odd + 2 * t)))

    send_rows(0)
    for_peers(lambda j: prob_copy(j).start())
    pick_rows(1)
    send_rows(1)
    load_stored.wait()
    quarter = rows // 4
    gates(0, quarter)
    gates(1, quarter)
    pick_rows(2)
    send_rows(2)
    gates(2, quarter)
    gates(3, quarter)
    pick_rows(3)
    pick_rows(4)
    row_at = lax.broadcasted_iota(jnp.int32, (rows, OWNERS * PAD), 0).astype(F32)
    padded_at = row_at + float(PAD - cap) * jnp.floor((row_at + 0.5) * (1.0 / cap))
    compact[...] = jnp.where(
        lax.broadcasted_iota(jnp.int32, (rows, OWNERS * PAD), 1).astype(F32) == padded_at, 1.0, 0.0
    ).astype(BF16)
    acc_in[0, 0] = jnp.zeros(acc_in.shape[2:], BF16)
    acc_in[1, 1] = jnp.zeros(acc_in.shape[2:], BF16)
    leaf_in[0, 0] = jnp.zeros(leaf_in.shape[2:], BF16)
    send_rows(3)
    for_peers(lambda j: prob_copy(j).wait_recv())
    prob_col[...] = jnp.dot(
        compact[...], prob_in[...].reshape(OWNERS * PAD, HALF), preferred_element_type=F32
    )
    back[...] = jnp.zeros_like(back)

    def early(i, carry):
        stage_e(i)
        return carry

    lax.fori_loop(0, 3, early, 0)
    send_rows(4)
    sib_copy(0).wait_recv()

    def turn(t, carry):
        sib_copy(t + 1).wait_recv()
        ring_step(t)

        @pl.when(t < 3)
        def _():
            pick_rows(t + 5)
            send_rows(t + 5)

        @pl.when(t < 5)
        def _():
            stage_e(t + 3)

        add_back(t)
        return carry

    lax.fori_loop(0, 6, turn, 0)
    add_back(6)
    sib_copy(7).wait_recv()
    ring_step(6)
    add_back(7)

    products = jnp.sum(hidden[...].astype(F32) * back[...], axis=1, keepdims=True)
    row_at = lax.broadcasted_iota(jnp.int32, (rows, HALF), 0).astype(F32)
    row_slot = row_at - float(cap) * jnp.floor((row_at + 0.5) * (1.0 / cap))
    lane_at = lax.broadcasted_iota(jnp.int32, (rows, HALF), 1).astype(F32)
    spread = jnp.where(lane_at == row_slot, jnp.broadcast_to(products, (rows, HALF)), 0.0)
    src_at = jnp.floor((lax.broadcasted_iota(jnp.int32, (OWNERS, rows), 1).astype(F32) + 0.5) * (1.0 / cap))
    gather = jnp.where(src_at == lax.broadcasted_iota(jnp.int32, (OWNERS, rows), 0).astype(F32), 1.0, 0.0)
    by_source = jnp.dot(gather, spread, preferred_element_type=F32, precision=lax.Precision.HIGHEST)
    for s in range(OWNERS):
        prod_out[s] = jnp.broadcast_to(by_source[s : s + 1], (8, HALF))
    prod_in[me] = prod_out[me]
    for_peers(lambda j: prod_copy(j).start())

    def finish_rows(b, size):
        at = pl.ds(b * size, size)
        scale = jnp.concatenate([prob_col[at, :]] * (hid_n // HALF), axis=1)
        grad = scale * back[at, :]
        pre[at, :hid_n] = (grad * d_gate[at, :]).astype(BF16)
        pre[at, hid_n:] = (grad * d_up[at, :]).astype(BF16)

    def store_pre(b, size):
        at = pl.ds(b * size, size)
        return pltpu.make_async_copy(pre.at[at], pre_hbm.at[at], sem_pre.at[b])

    half_rows = rows // 2
    finish_rows(0, half_rows)
    store_pre(0, half_rows).start()
    ring_step(7)
    finish_rows(1, half_rows)
    store_pre(1, half_rows).start()

    for_peers(lambda j: prod_copy(j).wait_recv())
    sub16 = lax.broadcasted_iota(jnp.int32, (OWNERS, HALF), 0)
    by_owner = jnp.zeros((OWNERS, HALF), F32)
    for e in range(OWNERS):
        by_owner = jnp.where(sub16 == e, jnp.broadcast_to(prod_in[e, 0:1, :], (OWNERS, HALF)), by_owner)
    by_slot = jnp.concatenate([by_owner, jnp.zeros((HALF - OWNERS, HALF), F32)], axis=0).T
    result = jnp.zeros((top, tok), F32)
    for e in range(OWNERS):
        match = jnp.broadcast_to(slots[e : e + 1], (PAD, tok)) == slot_at
        value = jnp.sum(
            jnp.where(match, jnp.broadcast_to(by_slot[0:PAD, e : e + 1], (PAD, tok)), 0.0), axis=0, keepdims=True
        )
        result = jnp.where(ids == e, jnp.broadcast_to(value, (top, tok)), result)
    gprobs_ref[...] = result

    def drain(i, carry):
        for_peers(lambda j: row_copy(i, j).wait_send())
        sib_copy(i).wait_send()
        return carry

    lax.fori_loop(0, CHUNKS, drain, 0)
    for_peers(lambda j: prob_copy(j).wait_send())
    for_peers(lambda j: prod_copy(j).wait_send())
    for way in range(2):

        def drain_ring(t, carry):
            for k in range(SUBS):
                hop(way, t, k).wait_send()
            return carry

        def drain_leaf(t, carry):
            leaf(way, t).wait_send()
            return carry

        lax.fori_loop(way, STEPS - 1, drain_ring, 0)
        lax.fori_loop(0, STEPS - 1, drain_leaf, 0)

    own = chip_slot(odd - REACH)
    piece = SHARE // SUBS
    for way in range(2):
        leaf(way, STEPS - 1).wait_recv()
    for k in range(SUBS):
        for way in range(2):
            hop(way, STEPS - 1, k).wait_recv()
        down_ref[0, k * piece : (k + 1) * piece, :] = (
            (acc_in[0, STEPS, k].astype(F32) + acc_in[1, STEPS, k].astype(F32))
            + (leaf_in[0, STEPS, k].astype(F32) + leaf_in[1, STEPS, k].astype(F32))
            + local_sum(own, k)
        )

    for way in range(2):
        leaf(way, STEPS - 1).wait_send()
        for k in range(SUBS):
            hop(way, STEPS - 1, k).wait_send()
    store_pre(0, half_rows).wait()
    store_pre(1, half_rows).wait()


PIECES = 7


def hand_on(down_in, pre_in, gprobs_in, down_out, pre_out, gprobs_out, down_buf, pre_buf, gprobs_buf, sems_in, sems_out):
    size = pre_in.shape[0] // PIECES
    trips = [
        (pre_in.at[pl.ds(b * size, size)], pre_buf.at[pl.ds(b * size, size)], pre_out.at[pl.ds(b * size, size)])
        for b in range(PIECES)
    ]
    trips += [(down_in, down_buf, down_out), (gprobs_in, gprobs_buf, gprobs_out)]
    reads = [pltpu.make_async_copy(src, buf, sems_in.at[n]) for n, (src, buf, _) in enumerate(trips)]
    writes = [pltpu.make_async_copy(buf, dst, sems_out.at[n]) for n, (_, buf, dst) in enumerate(trips)]
    for read in reads:
        read.start()
    for read, write in zip(reads, writes):
        read.wait()
        write.start()
    for write in writes:
        write.wait()


def local(out_grad, probs, expert_ids, saved_pre, down_weight):
    top, tok = expert_ids.shape[1], expert_ids.shape[0]
    rows, pre_n = saved_pre.shape
    hid_n = pre_n // 2
    piece = SHARE // SUBS
    dma = pltpu.SemaphoreType.DMA
    scratch = [
        pltpu.VMEM((CHUNKS, tok, WIDTH), BF16),
        pltpu.VMEM((CHUNKS, WIDTH, hid_n), BF16),
        pltpu.VMEM((rows, pre_n), BF16),
        pltpu.VMEM((rows, hid_n), BF16),
        pltpu.VMEM((rows, hid_n), F32),
        pltpu.VMEM((rows, hid_n), F32),
        pltpu.VMEM((rows, hid_n), F32),
        pltpu.VMEM((CHUNKS, rows, WIDTH), BF16),
        pltpu.VMEM((rows, pre_n), BF16),
        pltpu.VMEM((OWNERS * PAD, tok), BF16),
        pltpu.VMEM((CHUNKS, OWNERS, PAD, WIDTH), BF16),
        pltpu.VMEM((CHUNKS, OWNERS, PAD, WIDTH), BF16),
        pltpu.VMEM((OWNERS, PAD, HALF), BF16),
        pltpu.VMEM((OWNERS, PAD, HALF), BF16),
        pltpu.VMEM((rows, OWNERS * PAD), BF16),
        pltpu.VMEM((rows, HALF), F32),
        pltpu.VMEM((OWNERS, 8, HALF), F32),
        pltpu.VMEM((OWNERS, 8, HALF), F32),
        pltpu.VMEM((CHIPS, 2, SUBS, piece, hid_n), BF16),
        pltpu.VMEM((CHIPS, SUBS, piece, hid_n), BF16),
        pltpu.VMEM((2, STEPS, SUBS, piece, hid_n), BF16),
        pltpu.VMEM((2, STEPS + 1, SUBS, piece, hid_n), BF16),
        pltpu.VMEM((2, STEPS, SUBS, piece, hid_n), BF16),
        pltpu.VMEM((2, STEPS + 1, SUBS, piece, hid_n), BF16),
        dma((CHUNKS, 2)), dma((CHUNKS, 2)), dma, dma((2,)),
        dma((CHUNKS, OWNERS)), dma((CHUNKS, OWNERS)),
        dma((OWNERS,)), dma((OWNERS,)), dma((OWNERS,)), dma((OWNERS,)),
        dma((CHUNKS,)), dma((CHUNKS,)),
        dma((2, STEPS, SUBS)), dma((2, STEPS, SUBS)), dma((2, STEPS)), dma((2, STEPS)),
    ]
    hbm = pl.BlockSpec(memory_space=pl.ANY)
    vmem = pl.BlockSpec(memory_space=pltpu.VMEM)
    down, pre, gprobs = pl.pallas_call(
        kernel,
        out_shape=(
            jax.ShapeDtypeStruct((1, SHARE, hid_n), F32),
            jax.ShapeDtypeStruct((rows, pre_n), BF16),
            jax.ShapeDtypeStruct((top, tok), F32),
        ),
        in_specs=[hbm, vmem, vmem, hbm, hbm],
        out_specs=(vmem, hbm, vmem),
        scratch_shapes=scratch,
        compiler_params=pltpu.CompilerParams(
            collective_id=0, has_side_effects=True, vmem_limit_bytes=56 * 1024 * 1024
        ),
    )(out_grad, probs.T, expert_ids.T, saved_pre, down_weight)
    down, pre, gprobs = pl.pallas_call(
        hand_on,
        out_shape=tuple(jax.ShapeDtypeStruct(a.shape, a.dtype) for a in (down, pre, gprobs)),
        in_specs=[hbm] * 3,
        out_specs=(hbm, hbm, hbm),
        scratch_shapes=[pltpu.VMEM(a.shape, a.dtype) for a in (down, pre, gprobs)]
        + [dma((PIECES + 2,)), dma((PIECES + 2,))],
        compiler_params=pltpu.CompilerParams(vmem_limit_bytes=56 * 1024 * 1024),
    )(down, pre, gprobs)
    return down, pre, gprobs.T


def solution(mesh):
    in_specs = (
        P(("dp", "expert"), None),
        P(("dp", "expert"), None),
        P(("dp", "expert"), None),
        P(("dp", "expert"), None),
        P("expert", None, None),
    )
    out_specs = (P("expert", "dp", None), P(("dp", "expert"), None), P(("dp", "expert"), None))
    return jax.shard_map(local, mesh=mesh, in_specs=in_specs, out_specs=out_specs, check_vma=False)
```

```python
import jax
import jax.numpy as jnp
from jax import lax
from jax.experimental import pallas as pl
from jax.experimental.pallas import tpu as pltpu
from jax.sharding import PartitionSpec as P

MESH = pl.DeviceIdType.MESH
F32, BF16 = jnp.float32, jnp.bfloat16
PAD = 32
OWNERS = 16
CHUNKS = 8
WIDTH = 256
HALF = 128
REACH = 16
STEPS = 8
CHIPS = 32
SHARE = 32
SUBS = 2


def div(a, b):
    return lax.div(jnp.int32(a), jnp.int32(b))


def rem(a, b):
    return lax.rem(jnp.int32(a), jnp.int32(b))


def kernel(
    grad_hbm, probs_ref, ids_ref, stored_hbm, weight_hbm,
    down_ref, pre_hbm, gprobs_ref,
    own_g, w, stored, hidden, d_gate, d_up, back, routed_all, pre,
    select, rows_out, rows_in, prob_out, prob_in, compact, prob_col,
    prod_out, prod_in, part, part_in, acc_out, acc_in, leaf_out, leaf_in,
    sem_g, sem_w, sem_stored, sem_pre, gs, gr, ps, pr, rs, rr, ss, sr, zs, zr, ls, lr,
):
    top, tok = ids_ref.shape
    rows = stored_hbm.shape[0]
    hid_n = weight_hbm.shape[2]
    cap = rows // OWNERS
    dp = lax.axis_index("dp")
    me = lax.axis_index("expert")
    z, core = div(dp, 2), rem(dp, 2)
    odd = rem(z, 2)
    first_group = div(z + REACH, 2)
    n_groups = 2 * CHUNKS
    near = [(rem(z + by, CHIPS) * 2 + core, me) for by in (1, CHIPS - 1)]
    far = [(rem(z + by, CHIPS) * 2 + core, me) for by in (2, CHIPS - 2)]
    sibling = (z * 2 + 1 - core, me)

    barrier = pltpu.get_barrier_semaphore()

    def greet(j, carry):
        pl.semaphore_signal(barrier, inc=1, device_id=(dp, rem(me + j, OWNERS)), device_id_type=MESH)
        return carry

    for target in (*near, *far, sibling):
        pl.semaphore_signal(barrier, inc=1, device_id=target, device_id_type=MESH)
    lax.fori_loop(1, OWNERS, greet, 0)

    def group_of(i, half):
        par = rem(i, 2)
        start = (1 - par) * i - par * (i + 1)
        return rem(first_group + start + half + 2 * n_groups, n_groups)

    def load_g(i, half):
        at = pl.multiple_of(group_of(i, half) * HALF, HALF)
        return pltpu.make_async_copy(
            grad_hbm.at[:, pl.ds(at, HALF)], own_g.at[i, :, pl.ds(half * HALF, HALF)], sem_g.at[i, half]
        )

    def load_w(i, half):
        at = pl.multiple_of(group_of(i, half) * HALF, HALF)
        return pltpu.make_async_copy(
            weight_hbm.at[0, pl.ds(at, HALF), :], w.at[i, pl.ds(half * HALF, HALF), :], sem_w.at[i, half]
        )

    for i in range(CHUNKS):
        for half in range(2):
            load_g(i, half).start()
    load_stored = pltpu.make_async_copy(stored_hbm, stored, sem_stored)
    load_stored.start()
    for i in range(CHUNKS):
        for half in range(2):
            load_w(i, half).start()

    ids = ids_ref[...]
    owner = lax.broadcasted_iota(jnp.int32, (OWNERS, tok), 0)
    chosen = jnp.zeros((OWNERS, tok), F32)
    prob = jnp.zeros((OWNERS, tok), F32)
    probs = probs_ref[...].astype(F32)
    for k in range(top):
        hit = jnp.broadcast_to(ids[k : k + 1], (OWNERS, tok)) == owner
        chosen = chosen + jnp.where(hit, 1.0, 0.0)
        prob = prob + jnp.where(hit, jnp.broadcast_to(probs[k : k + 1], (OWNERS, tok)), 0.0)
    earlier = (
        lax.broadcasted_iota(jnp.int32, (tok, tok), 0) < lax.broadcasted_iota(jnp.int32, (tok, tok), 1)
    )
    before = jnp.dot(
        chosen.astype(BF16), jnp.where(earlier, 1.0, 0.0).astype(BF16), preferred_element_type=F32
    )
    slots = jnp.where(chosen > 0.0, before, -1.0)
    slot_at = lax.broadcasted_iota(jnp.int32, (PAD, tok), 0).astype(F32)
    for e in range(OWNERS):
        match = jnp.broadcast_to(slots[e : e + 1], (PAD, tok)) == slot_at
        select[e * PAD : (e + 1) * PAD, :] = jnp.where(match, 1.0, 0.0).astype(BF16)
        filled = jnp.sum(
            jnp.where(match, jnp.broadcast_to(prob[e : e + 1], (PAD, tok)), 0.0), axis=1, keepdims=True
        )
        prob_out[e] = jnp.broadcast_to(filled, (PAD, HALF)).astype(BF16)

    def pick_rows(i):
        load_g(i, 0).wait()
        load_g(i, 1).wait()
        picked = jnp.dot(select[...], own_g[i], preferred_element_type=F32)
        rows_out[i] = picked.astype(BF16).reshape(OWNERS, PAD, WIDTH)
        rows_in[i, me] = rows_out[i, me]

    pick_rows(0)
    prob_in[me] = prob_out[me]
    pl.semaphore_wait(barrier, OWNERS - 1 + 5)

    def row_copy(i, j):
        other = rem(me + j, OWNERS)
        return pltpu.make_async_remote_copy(
            src_ref=rows_out.at[i, other], dst_ref=rows_in.at[i, me], send_sem=gs.at[i, j], recv_sem=gr.at[i, j],
            device_id=(dp, other), device_id_type=MESH,
        )

    def prob_copy(j):
        other = rem(me + j, OWNERS)
        return pltpu.make_async_remote_copy(
            src_ref=prob_out.at[other], dst_ref=prob_in.at[me], send_sem=ps.at[j], recv_sem=pr.at[j],
            device_id=(dp, other), device_id_type=MESH,
        )

    def prod_copy(j):
        other = rem(me + j, OWNERS)
        return pltpu.make_async_remote_copy(
            src_ref=prod_out.at[other], dst_ref=prod_in.at[me], send_sem=rs.at[j], recv_sem=rr.at[j],
            device_id=(dp, other), device_id_type=MESH,
        )

    def for_peers(act):
        def body(j, carry):
            act(j)
            return carry

        lax.fori_loop(1, OWNERS, body, 0)

    def send_rows(i):
        for_peers(lambda j: row_copy(i, j).start())

    def gates(b, size):
        at = pl.ds(b * size, size)
        a = stored[at, :hid_n].astype(F32)
        up = stored[at, hid_n:].astype(F32)
        sg = jax.nn.sigmoid(a)
        act = a * sg
        hidden[at, :] = (act * up).astype(BF16)
        d_gate[at, :] = up * sg * (1.0 + a * (1.0 - sg))
        d_up[at, :] = act

    def sib_copy(i):
        at = pl.ds(4 * i, 4)
        return pltpu.make_async_remote_copy(
            src_ref=part.at[at, 1 - core], dst_ref=part_in.at[at], send_sem=ss.at[i], recv_sem=sr.at[i],
            device_id=sibling, device_id_type=MESH,
        )

    def stage_e(i):
        for_peers(lambda j: row_copy(i, j).wait_recv())
        arrived = rows_in[i].reshape(OWNERS * PAD, WIDTH)
        routed = jnp.dot(compact[...], arrived, preferred_element_type=F32)
        routed_all[i] = routed.astype(BF16)
        weight_row = jnp.concatenate([prob_col[...], prob_col[...]], axis=1)
        scaled = (weight_row * routed).astype(BF16)
        summed = lax.dot_general(
            scaled, hidden[...], (((0,), (0,)), ((), ())), preferred_element_type=F32
        )
        part[pl.ds(4 * i, 4)] = summed.astype(BF16).reshape(4, 2, SUBS, SHARE // SUBS, hid_n)
        sib_copy(i).start()

    def add_back(i):
        for n in range(2):
            load_w(i + n, 0).wait()
            load_w(i + n, 1).wait()
        back[...] += jnp.dot(routed_all[i], w[i], preferred_element_type=F32) + jnp.dot(
            routed_all[i + 1], w[i + 1], preferred_element_type=F32
        )

    def chip_slot(off):
        at = off + REACH
        m = rem(div(at, 2), n_groups)
        high = div(m, CHUNKS)
        chunk = (1 - high) * (7 - 2 * div(m, 2)) + high * 2 * div(m - CHUNKS * high, 2)
        return 4 * chunk + 2 * rem(m, 2) + rem(at, 2)

    def hop(way, t, k):
        return pltpu.make_async_remote_copy(
            src_ref=acc_out.at[way, t, k], dst_ref=acc_in.at[way, t + 1, k],
            send_sem=zs.at[way, t, k], recv_sem=zr.at[way, t, k],
            device_id=far[way], device_id_type=MESH,
        )

    def leaf(way, t):
        return pltpu.make_async_remote_copy(
            src_ref=leaf_out.at[way, t], dst_ref=leaf_in.at[way, t + 1],
            send_sem=ls.at[way, t], recv_sem=lr.at[way, t],
            device_id=near[way], device_id_type=MESH,
        )

    def local_sum(slot, k):
        return part[slot, core, k].astype(F32) + part_in[slot, k].astype(F32)

    def guarded(condition, act):
        if isinstance(condition, bool):
            if condition:
                act()
        else:
            pl.when(condition)(act)

    def ring_step(t):
        for way in range(2):
            slot = chip_slot(odd - 2 * t - 1) if way == 0 else chip_slot(odd + 1 + 2 * t)
            for k in range(SUBS):
                leaf_out[way, t, k] = local_sum(slot, k).astype(BF16)
            leaf(way, t).start()

        def pass_on(way, k, slot):
            if k == 0:
                guarded(t > 0, lambda: leaf(way, t - 1).wait_recv())
            guarded(t > way, lambda: hop(way, t - 1, k).wait_recv())
            acc_out[way, t, k] = (
                acc_in[way, t, k].astype(F32) + leaf_in[way, t, k].astype(F32) + local_sum(slot, k)
            ).astype(BF16)
            hop(way, t, k).start()

        for k in range(SUBS):
            pass_on(0, k, chip_slot(odd - 2 * t))
            guarded(t > 0, lambda: pass_on(1, k, chip_slot(odd + 2 * t)))

    send_rows(0)
    for_peers(lambda j: prob_copy(j).start())
    pick_rows(1)
    send_rows(1)
    load_stored.wait()
    quarter = rows // 4
    gates(0, quarter)
    gates(1, quarter)
    pick_rows(2)
    send_rows(2)
    gates(2, quarter)
    gates(3, quarter)
    pick_rows(3)
    pick_rows(4)
    row_at = lax.broadcasted_iota(jnp.int32, (rows, OWNERS * PAD), 0).astype(F32)
    padded_at = row_at + float(PAD - cap) * jnp.floor((row_at + 0.5) * (1.0 / cap))
    compact[...] = jnp.where(
        lax.broadcasted_iota(jnp.int32, (rows, OWNERS * PAD), 1).astype(F32) == padded_at, 1.0, 0.0
    ).astype(BF16)
    acc_in[0, 0] = jnp.zeros(acc_in.shape[2:], BF16)
    acc_in[1, 1] = jnp.zeros(acc_in.shape[2:], BF16)
    leaf_in[0, 0] = jnp.zeros(leaf_in.shape[2:], BF16)
    send_rows(3)
    for_peers(lambda j: prob_copy(j).wait_recv())
    prob_col[...] = jnp.dot(
        compact[...], prob_in[...].reshape(OWNERS * PAD, HALF), preferred_element_type=F32
    )
    back[...] = jnp.zeros_like(back)

    def early(i, carry):
        stage_e(i)
        return carry

    lax.fori_loop(0, 3, early, 0)
    send_rows(4)
    sib_copy(0).wait_recv()

    def turn(t, carry):
        sib_copy(t + 1).wait_recv()
        ring_step(t)

        @pl.when(t < 3)
        def _():
            pick_rows(t + 5)
            send_rows(t + 5)

        @pl.when(t < 5)
        def _():
            stage_e(t + 3)

        @pl.when(rem(t, 2) == 1)
        def _():
            add_back(t - 1)

        return carry

    lax.fori_loop(0, 6, turn, 0)
    sib_copy(7).wait_recv()
    ring_step(6)
    add_back(6)

    products = jnp.sum(hidden[...].astype(F32) * back[...], axis=1, keepdims=True)
    row_at = lax.broadcasted_iota(jnp.int32, (rows, HALF), 0).astype(F32)
    row_slot = row_at - float(cap) * jnp.floor((row_at + 0.5) * (1.0 / cap))
    lane_at = lax.broadcasted_iota(jnp.int32, (rows, HALF), 1).astype(F32)
    spread = jnp.where(lane_at == row_slot, jnp.broadcast_to(products, (rows, HALF)), 0.0)
    src_at = jnp.floor((lax.broadcasted_iota(jnp.int32, (OWNERS, rows), 1).astype(F32) + 0.5) * (1.0 / cap))
    gather = jnp.where(src_at == lax.broadcasted_iota(jnp.int32, (OWNERS, rows), 0).astype(F32), 1.0, 0.0)
    by_source = jnp.dot(gather, spread, preferred_element_type=F32, precision=lax.Precision.HIGHEST)
    for s in range(OWNERS):
        prod_out[s] = jnp.broadcast_to(by_source[s : s + 1], (8, HALF))
    prod_in[me] = prod_out[me]
    for_peers(lambda j: prod_copy(j).start())

    def finish_rows(b, size):
        at = pl.ds(b * size, size)
        scale = jnp.concatenate([prob_col[at, :]] * (hid_n // HALF), axis=1)
        grad = scale * back[at, :]
        pre[at, :hid_n] = (grad * d_gate[at, :]).astype(BF16)
        pre[at, hid_n:] = (grad * d_up[at, :]).astype(BF16)

    def store_pre(b, size):
        at = pl.ds(b * size, size)
        return pltpu.make_async_copy(pre.at[at], pre_hbm.at[at], sem_pre.at[b])

    half_rows = rows // 2
    finish_rows(0, half_rows)
    store_pre(0, half_rows).start()
    ring_step(7)
    finish_rows(1, half_rows)
    store_pre(1, half_rows).start()

    for_peers(lambda j: prod_copy(j).wait_recv())
    sub16 = lax.broadcasted_iota(jnp.int32, (OWNERS, HALF), 0)
    by_owner = jnp.zeros((OWNERS, HALF), F32)
    for e in range(OWNERS):
        by_owner = jnp.where(sub16 == e, jnp.broadcast_to(prod_in[e, 0:1, :], (OWNERS, HALF)), by_owner)
    by_slot = jnp.concatenate([by_owner, jnp.zeros((HALF - OWNERS, HALF), F32)], axis=0).T
    result = jnp.zeros((top, tok), F32)
    for e in range(OWNERS):
        match = jnp.broadcast_to(slots[e : e + 1], (PAD, tok)) == slot_at
        value = jnp.sum(
            jnp.where(match, jnp.broadcast_to(by_slot[0:PAD, e : e + 1], (PAD, tok)), 0.0), axis=0, keepdims=True
        )
        result = jnp.where(ids == e, jnp.broadcast_to(value, (top, tok)), result)
    gprobs_ref[...] = result

    def drain(i, carry):
        for_peers(lambda j: row_copy(i, j).wait_send())
        sib_copy(i).wait_send()
        return carry

    lax.fori_loop(0, CHUNKS, drain, 0)
    for_peers(lambda j: prob_copy(j).wait_send())
    for_peers(lambda j: prod_copy(j).wait_send())
    for way in range(2):

        def drain_ring(t, carry):
            for k in range(SUBS):
                hop(way, t, k).wait_send()
            return carry

        def drain_leaf(t, carry):
            leaf(way, t).wait_send()
            return carry

        lax.fori_loop(way, STEPS - 1, drain_ring, 0)
        lax.fori_loop(0, STEPS - 1, drain_leaf, 0)

    own = chip_slot(odd - REACH)
    piece = SHARE // SUBS
    for way in range(2):
        leaf(way, STEPS - 1).wait_recv()
    for k in range(SUBS):
        for way in range(2):
            hop(way, STEPS - 1, k).wait_recv()
        down_ref[0, k * piece : (k + 1) * piece, :] = (
            (acc_in[0, STEPS, k].astype(F32) + acc_in[1, STEPS, k].astype(F32))
            + (leaf_in[0, STEPS, k].astype(F32) + leaf_in[1, STEPS, k].astype(F32))
            + local_sum(own, k)
        )

    for way in range(2):
        leaf(way, STEPS - 1).wait_send()
        for k in range(SUBS):
            hop(way, STEPS - 1, k).wait_send()
    store_pre(0, half_rows).wait()
    store_pre(1, half_rows).wait()


PIECES = 7


def hand_on(down_in, pre_in, gprobs_in, down_out, pre_out, gprobs_out, down_buf, pre_buf, gprobs_buf, sems_in, sems_out):
    size = pre_in.shape[0] // PIECES
    trips = [
        (pre_in.at[pl.ds(b * size, size)], pre_buf.at[pl.ds(b * size, size)], pre_out.at[pl.ds(b * size, size)])
        for b in range(PIECES)
    ]
    trips += [(down_in, down_buf, down_out), (gprobs_in, gprobs_buf, gprobs_out)]
    reads = [pltpu.make_async_copy(src, buf, sems_in.at[n]) for n, (src, buf, _) in enumerate(trips)]
    writes = [pltpu.make_async_copy(buf, dst, sems_out.at[n]) for n, (_, buf, dst) in enumerate(trips)]
    for read in reads:
        read.start()
    for read, write in zip(reads, writes):
        read.wait()
        write.start()
    for write in writes:
        write.wait()


def local(out_grad, probs, expert_ids, saved_pre, down_weight):
    top, tok = expert_ids.shape[1], expert_ids.shape[0]
    rows, pre_n = saved_pre.shape
    hid_n = pre_n // 2
    piece = SHARE // SUBS
    dma = pltpu.SemaphoreType.DMA
    scratch = [
        pltpu.VMEM((CHUNKS, tok, WIDTH), BF16),
        pltpu.VMEM((CHUNKS, WIDTH, hid_n), BF16),
        pltpu.VMEM((rows, pre_n), BF16),
        pltpu.VMEM((rows, hid_n), BF16),
        pltpu.VMEM((rows, hid_n), F32),
        pltpu.VMEM((rows, hid_n), F32),
        pltpu.VMEM((rows, hid_n), F32),
        pltpu.VMEM((CHUNKS, rows, WIDTH), BF16),
        pltpu.VMEM((rows, pre_n), BF16),
        pltpu.VMEM((OWNERS * PAD, tok), BF16),
        pltpu.VMEM((CHUNKS, OWNERS, PAD, WIDTH), BF16),
        pltpu.VMEM((CHUNKS, OWNERS, PAD, WIDTH), BF16),
        pltpu.VMEM((OWNERS, PAD, HALF), BF16),
        pltpu.VMEM((OWNERS, PAD, HALF), BF16),
        pltpu.VMEM((rows, OWNERS * PAD), BF16),
        pltpu.VMEM((rows, HALF), F32),
        pltpu.VMEM((OWNERS, 8, HALF), F32),
        pltpu.VMEM((OWNERS, 8, HALF), F32),
        pltpu.VMEM((CHIPS, 2, SUBS, piece, hid_n), BF16),
        pltpu.VMEM((CHIPS, SUBS, piece, hid_n), BF16),
        pltpu.VMEM((2, STEPS, SUBS, piece, hid_n), BF16),
        pltpu.VMEM((2, STEPS + 1, SUBS, piece, hid_n), BF16),
        pltpu.VMEM((2, STEPS, SUBS, piece, hid_n), BF16),
        pltpu.VMEM((2, STEPS + 1, SUBS, piece, hid_n), BF16),
        dma((CHUNKS, 2)), dma((CHUNKS, 2)), dma, dma((2,)),
        dma((CHUNKS, OWNERS)), dma((CHUNKS, OWNERS)),
        dma((OWNERS,)), dma((OWNERS,)), dma((OWNERS,)), dma((OWNERS,)),
        dma((CHUNKS,)), dma((CHUNKS,)),
        dma((2, STEPS, SUBS)), dma((2, STEPS, SUBS)), dma((2, STEPS)), dma((2, STEPS)),
    ]
    hbm = pl.BlockSpec(memory_space=pl.ANY)
    vmem = pl.BlockSpec(memory_space=pltpu.VMEM)
    down, pre, gprobs = pl.pallas_call(
        kernel,
        out_shape=(
            jax.ShapeDtypeStruct((1, SHARE, hid_n), F32),
            jax.ShapeDtypeStruct((rows, pre_n), BF16),
            jax.ShapeDtypeStruct((top, tok), F32),
        ),
        in_specs=[hbm, vmem, vmem, hbm, hbm],
        out_specs=(vmem, hbm, vmem),
        scratch_shapes=scratch,
        compiler_params=pltpu.CompilerParams(
            collective_id=0, has_side_effects=True, vmem_limit_bytes=56 * 1024 * 1024
        ),
    )(out_grad, probs.T, expert_ids.T, saved_pre, down_weight)
    down, pre, gprobs = pl.pallas_call(
        hand_on,
        out_shape=tuple(jax.ShapeDtypeStruct(a.shape, a.dtype) for a in (down, pre, gprobs)),
        in_specs=[hbm] * 3,
        out_specs=(hbm, hbm, hbm),
        scratch_shapes=[pltpu.VMEM(a.shape, a.dtype) for a in (down, pre, gprobs)]
        + [dma((PIECES + 2,)), dma((PIECES + 2,))],
        compiler_params=pltpu.CompilerParams(vmem_limit_bytes=56 * 1024 * 1024),
    )(down, pre, gprobs)
    return down, pre, gprobs.T


def solution(mesh):
    in_specs = (
        P(("dp", "expert"), None),
        P(("dp", "expert"), None),
        P(("dp", "expert"), None),
        P(("dp", "expert"), None),
        P("expert", None, None),
    )
    out_specs = (P("expert", "dp", None), P(("dp", "expert"), None), P(("dp", "expert"), None))
    return jax.shard_map(local, mesh=mesh, in_specs=in_specs, out_specs=out_specs, check_vma=False)
```
